32 devices in a mesh: row: 4 (over y, core), col: 8 (over z, x).
Axes of the slice: x: 2, y: 2, z: 4, core: 2. Of those that a mesh axis runs over, the one named last changes fastest.
Arguments:
- hidden_in: bfloat16 [16384, 1024], P(('row', 'col')), may hold values from -6 to 6
- cotangent: float32 [16384, 1024], P(('row', 'col')), may hold values from -6 to 6
- seq_lengths: int32 [16], replicated, may hold values from 1 to 1024, 10240 in all
- slot_of: int32 [16], replicated, may hold values from 0 to 15, each once
- project: bfloat16 [2, 1024, 3072], P(None, 'row', 'col'), may hold values from -0.1875 to 0.1875
- offsets: float32 [2, 2048], P(None, 'col'), may hold values from -1.5 to 1.5
- combiner: bfloat16 [2, 1024, 1024], P(None, 'col', 'row'), may hold values from -1.5 to 1.5
- recenter: float32 [2, 1024], replicated, may hold values from -1.5 to 1.5
- stretch: float32 [2, 1024], replicated, may hold values from 0.5 to 1.5
- displace: float32 [2, 1024], replicated, may hold values from -1.5 to 1.5
- expand: bfloat16 [2, 1024, 4096], P(None, 'row', 'col'), may hold values from -0.1875 to 0.1875
- uplift: float32 [2, 4096], P(None, 'col'), may hold values from -1.5 to 1.5
- shrink: bfloat16 [2, 4096, 1024], P(None, 'col', 'row'), may hold values from -0.09375 to 0.09375
- lowering: float32 [2, 1024], replicated, may hold values from -1.5 to 1.5
- restretch: float32 [2, 1024], replicated, may hold values from 0.5 to 1.5
- redisplace: float32 [2, 1024], replicated, may hold values from -1.5 to 1.5
Outputs:
- hidden_out: float32 [16384, 1024], P(('row', 'col'))
- hidden_grad: float32 [16384, 1024], P(('row', 'col'))
- project_grad: float32 [2, 1024, 3072], P(None, 'row', 'col')
- offsets_grad: float32 [2, 2048], P(None, 'col')
- combiner_grad: float32 [2, 1024, 1024], P(None, 'col', 'row')
- recenter_grad: float32 [2, 1024], replicated
- stretch_grad: float32 [2, 1024], replicated
- displace_grad: float32 [2, 1024], replicated
- expand_grad: float32 [2, 1024, 4096], P(None, 'row', 'col')
- uplift_grad: float32 [2, 4096], P(None, 'col')
- shrink_grad: float32 [2, 4096, 1024], P(None, 'col', 'row')
- lowering_grad: float32 [2, 1024], replicated
- restretch_grad: float32 [2, 1024], replicated
- redisplace_grad: float32 [2, 1024], replicated
The draws below stay inside these ranges and needn't reach their ends.
Inputs may be any that keep to these rules, and one draw needn't show every extreme that they name: `slot_of`: slot j holds tokens j * 1024 to (j + 1) * 1024 - 1 and lies on row index j // 4; every slot holds exactly one sequence. `seq_lengths`: a sequence's live tokens stand at the start of its slot; the lengths sum to 10240.
All inputs are finite; a program needn't handle non-finite values.
Results may differ from the reference program's by a relative error of at most 0.03.
Values may be sent and summed in bfloat16 or wider, within the bound.
No kernel may reach another device: no remote copies, remote signals or barrier semaphores. Data moves between devices by JAX's collectives and lax.ppermute only.
A program may use at most 256 MiB of HBM per device.

```python
import math
import jax
import jax.numpy as jnp
import numpy as np
from jax import lax

D = 1024
FF = 4096
HEADS = 16
HEAD_DIM = 64
LAYERS = 2
SLOT = 1024
SEQS = 16
TOKENS = 16384
LIVE = 10240


def block_levels(own_key, dims, shards, low, top_value):
    def one(position, blocks):
        heights = jax.random.uniform(jax.random.fold_in(jax.random.fold_in(own_key, 6), position), (blocks,), jnp.float32, low / len(shards), top_value / len(shards))
        return jnp.repeat(jnp.exp(heights), dims[position] // blocks).reshape((-1,) + (1,) * (len(dims) - position - 1))

    loudness = one(*shards[0])
    for cut in shards[1:]:
        loudness = loudness * one(*cut)
    return loudness


def profile(number_of, total, most, skew):
    weights = [(1 << 20) // math.isqrt(standing ** skew) + 1 for standing in range(2, number_of + 1)]
    spare, given = total - most - (number_of - 1), [1] * (number_of - 1)
    while spare > 0:
        free = [i for i in range(number_of - 1) if given[i] < most]
        mass, remaining = sum([weights[i] for i in free]), spare
        for i in free:
            addition = min(most - given[i], max(1, remaining * weights[i] // mass), spare)
            given[i] = given[i] + addition
            spare = spare - addition
    return np.array([most] + given)


def ragged_sizes(own_key, number_of, total, limit, slope):
    if number_of == 2:
        one = jax.random.randint(own_key, (), max(1, total - limit), min(limit, total - 1) + 1)
        return jnp.stack([one, total - one])
    sizes = jnp.asarray(profile(number_of, total, limit, slope), jnp.int32)
    twos = (number_of - 1) // 2
    giver, taker = sizes[1:1 + 2 * twos:2], sizes[2:2 + 2 * twos:2]
    margin = jnp.minimum(giver - 1, limit - taker)
    passed = jax.random.randint(jax.random.fold_in(own_key, 1), (twos,), 0, 1 << 20) % (margin + 1)
    sizes = sizes.at[1:1 + 2 * twos:2].set(giver - passed).at[2:2 + 2 * twos:2].set(taker + passed)
    return sizes[jax.random.permutation(jax.random.fold_in(own_key, 2), number_of)]


def scatter_about(key, dims, deviation, most, cuts=(), kind=jnp.bfloat16):
    entries = deviation * jax.random.normal(key, dims, jnp.float32)
    if cuts:
        entries = entries * block_levels(key, dims, cuts, -0.22, 0.18)
    return jnp.clip(entries, -most, most).astype(kind)


def setup_inputs(seed: int = 0) -> dict:
    seeds = jax.random.split(jax.random.key(seed), 17)
    return {
        "hidden_in": scatter_about(seeds[0], (TOKENS, D), 1.0, 6.0, ((0, 32),)),
        "cotangent": scatter_about(seeds[1], (TOKENS, D), 1.0, 6.0, ((0, 32),), jnp.float32),
        "seq_lengths": ragged_sizes(seeds[2], SEQS, LIVE, SLOT, 2).astype(jnp.int32),
        "slot_of": jax.random.permutation(seeds[3], SEQS).astype(jnp.int32),
        "project": scatter_about(seeds[4], (LAYERS, D, 3 * D), D ** -0.5, 0.1875, ((1, 4), (2, 8))),
        "offsets": scatter_about(seeds[5], (LAYERS, 2 * D), 0.3, 1.5, ((1, 8),), jnp.float32),
        "combiner": scatter_about(seeds[6], (LAYERS, D, D), (D // 64) ** -0.5, 1.5, ((1, 8), (2, 4))),
        "recenter": scatter_about(seeds[7], (LAYERS, D), 0.3, 1.5, (), jnp.float32),
        "stretch": jnp.clip(1.0 + 0.1 * jax.random.normal(seeds[8], (LAYERS, D), jnp.float32), 0.5, 1.5),
        "displace": scatter_about(seeds[9], (LAYERS, D), 0.3, 1.5, (), jnp.float32),
        "expand": scatter_about(seeds[10], (LAYERS, D, FF), D ** -0.5, 0.1875, ((1, 4), (2, 8))),
        "uplift": scatter_about(seeds[11], (LAYERS, FF), 0.3, 1.5, ((1, 8),), jnp.float32),
        "shrink": scatter_about(seeds[12], (LAYERS, FF, D), FF ** -0.5, 0.09375, ((1, 8), (2, 4))),
        "lowering": scatter_about(seeds[13], (LAYERS, D), 0.3, 1.5, (), jnp.float32),
        "restretch": jnp.clip(1.0 + 0.1 * jax.random.normal(seeds[14], (LAYERS, D), jnp.float32), 0.5, 1.5),
        "redisplace": scatter_about(seeds[15], (LAYERS, D), 0.3, 1.5, (), jnp.float32),
    }


@jax.custom_vjp
def low(v):
    return lax.optimization_barrier(v.astype(jnp.bfloat16)).astype(jnp.float32)

@jax.custom_vjp
def low_back(v):
    return v

def low_keep(v):
    return (low(v), None)

def low_pass(kept, grad):
    return (grad,)

def back_keep(v):
    return (v, None)

def back_low(kept, grad):
    return (low(grad),)
low.defvjp(low_keep, low_pass)
low_back.defvjp(back_keep, back_low)

def matmul(left, right):
    return jnp.dot(left, right, precision=lax.Precision.HIGHEST, preferred_element_type=jnp.float32)

def layer_norm(summed, gain, shift):
    center = lax.optimization_barrier(jnp.mean(summed, axis=-1, keepdims=True))
    offset = summed - center
    spread = lax.optimization_barrier(jnp.mean(offset * offset, axis=-1, keepdims=True))
    return offset * lax.rsqrt(spread + 1e-12) * gain + shift

def attend(pieces):
    queries, keys, values, length = pieces
    usable = jnp.arange(SLOT, dtype=jnp.int32) < length
    scores = jnp.einsum('qhe,khe->hqk', queries, keys, precision=lax.Precision.HIGHEST) * (1.0 / math.sqrt(HEAD_DIM))
    scores = jnp.where(usable[None, None, :], low_back(scores), -1e+30)
    probs = low(jax.nn.softmax(scores, axis=-1))
    context = jnp.einsum('hqk,khe->qhe', probs, values, precision=lax.Precision.HIGHEST)
    return low(low_back(context))

def forward(current, slot_len, project, offsets, combiner, recenter, stretch, displace, expand, uplift, shrink, lowering, restretch, redisplace):
    shaped = (SEQS, SLOT, HEADS, HEAD_DIM)
    for layer_index in range(LAYERS):
        mixed = matmul(low(current), project[layer_index]).reshape(TOKENS, HEADS, 3, HEAD_DIM)
        paired = offsets[layer_index].reshape(HEADS, 2, HEAD_DIM)
        queries = low(low_back(mixed[:, :, 0] + paired[:, 0]))
        keys = low(low_back(mixed[:, :, 1]))
        values = low(low_back(mixed[:, :, 2] + paired[:, 1]))
        context = lax.map(jax.checkpoint(attend), (queries.reshape(shaped), keys.reshape(shaped), values.reshape(shaped), slot_len))
        branch = low_back(matmul(context.reshape(TOKENS, D), combiner[layer_index]) + recenter[layer_index])
        normed = layer_norm(current + branch, stretch[layer_index], displace[layer_index])
        inner = low_back(matmul(low(normed), expand[layer_index]) + uplift[layer_index])
        active = low(jax.nn.gelu(inner, approximate=False))
        branch_two = low_back(matmul(active, shrink[layer_index]) + lowering[layer_index])
        current = layer_norm(normed + branch_two, restretch[layer_index], redisplace[layer_index])
    return current

def reference(hidden_in, cotangent, seq_lengths, slot_of, project, offsets, combiner, recenter, stretch, displace, expand, uplift, shrink, lowering, restretch, redisplace):
    slot_len = jnp.zeros((SEQS,), jnp.int32).at[slot_of].set(seq_lengths)
    params = tuple((tensor.astype(jnp.float32) for tensor in (project, offsets, combiner, recenter, stretch, displace, expand, uplift, shrink, lowering, restretch, redisplace)))

    def run(current, *weights):
        return forward(current, slot_len, *weights)
    hidden_out, pull = jax.vjp(run, hidden_in.astype(jnp.float32), *params)
    grads = pull(cotangent.astype(jnp.float32))
    return (hidden_out, grads[0], grads[1], grads[2], grads[3], grads[4], grads[5], grads[6], grads[7], grads[8], grads[9], grads[10], grads[11], grads[12])
```

```python
import functools
import math

import jax
import jax.numpy as jnp
from jax import lax
from jax.experimental import pallas as pl
from jax.experimental.pallas import tpu as pltpu
from jax.sharding import Mesh, PartitionSpec as P

HEADS = 16
HEAD_DIM = 64
LAYERS = 2
DEPTH = 4

EPSILON = 1e-12
NEGATIVE = -1e30
SQRT_HALF = 0.7071067811865476
ROOT_TWO_PI_INV = 0.3989422804014327
FACTOR = 1.0 / math.sqrt(HEAD_DIM)
VMEM = 52 * 1024 * 1024
F32 = jnp.float32
BF16 = jnp.bfloat16
NT = (((1,), (1,)), ((), ()))
NN = (((1,), (0,)), ((), ()))
ANY_AXES = ("y", "core", "z", "x")


def dot(left, right, dims=NN):
    return lax.dot_general(left, right, dims, preferred_element_type=F32)


def pull(value, axis, step):
    size = lax.axis_size(axis)
    return lax.ppermute(value, axis, [(i, (i + step) % size) for i in range(size)])


def push(value, axis, step):
    size = lax.axis_size(axis)
    return lax.ppermute(value, axis, [(i, (i - step) % size) for i in range(size)])


def spread(value, axis):
    return [value] + [pull(value, axis, s) for s in range(1, lax.axis_size(axis))]


def collect(pieces, axis):
    total = pieces[0].astype(F32)
    for s in range(1, lax.axis_size(axis)):
        total = total + push(pieces[s], axis, s).astype(F32)
    return total


def gather_weight(block, order):
    value = jnp.stack(spread(block, "z"))
    value = jnp.stack(spread(value, order[0]))
    own = spread(value, order[1])
    return own + [pull(piece, "core", 1) for piece in own]


def scatter_weight(pieces, order):
    value = collect(pieces, order[1]).astype(BF16)
    value = collect([value[s] for s in range(value.shape[0])], order[0]).astype(BF16)
    return collect([value[s] for s in range(value.shape[0])], "z")


def relative_blocks(value, axes):
    sizes = [lax.axis_size(axis) for axis in axes]
    count = math.prod(sizes)
    width = value.shape[-1] // count
    parts = []
    for place in range(count):
        low = place % sizes[1]
        high = place // sizes[1]
        source = ((lax.axis_index(axes[0]) - high) % sizes[0]) * sizes[1] + (
            lax.axis_index(axes[1]) - low
        ) % sizes[1]
        parts.append(lax.dynamic_slice_in_dim(value, source * width, width, value.ndim - 1))
    return jnp.concatenate(parts, axis=-1)


def tile(refs, order, core, y, x):
    half = len(refs) // 2
    if order[1] == "x":
        return refs[core * half + x][y, 0]
    return refs[core * half + y][x, 0]


def input_slab(refs, order, ys, xs):
    return jnp.concatenate(
        [
            jnp.concatenate([tile(refs, order, core, y, x) for x in range(xs)], axis=1)
            for y in range(ys)
            for core in range(2)
        ],
        axis=0,
    )


def output_slab(refs, order, ys, xs):
    return jnp.concatenate(
        [
            jnp.concatenate(
                [tile(refs, order, core, y, x) for y in range(ys) for core in range(2)], axis=1
            )
            for x in range(xs)
        ],
        axis=0,
    )


def weight_specs(weights):
    return [
        pl.BlockSpec((w.shape[0], 1, w.shape[2], w.shape[3]), lambda z: (0, z, 0, 0))
        for w in weights
    ]


def whole(value):
    return pl.BlockSpec(value.shape, lambda z: (0,) * len(value.shape))


def by_z(rows, columns):
    return pl.BlockSpec((rows, columns // DEPTH), lambda z: (0, z))


def params():
    return pltpu.CompilerParams(vmem_limit_bytes=VMEM, dimension_semantics=("arbitrary",))


def cost(flops, arrays, special=0):
    return pl.CostEstimate(
        flops=flops,
        bytes_accessed=sum(a.size * a.dtype.itemsize for a in arrays),
        transcendentals=special,
    )


def weight_size(weights):
    return sum(w.size for w in weights)


def queries_kernel(order, ys, xs, x_ref, bias_ref, *refs):
    weights, (q_ref, k_ref, v_ref) = (refs[:-3], refs[-3:])
    mixed = dot(x_ref[...], input_slab(weights, order, ys, xs))
    wide = q_ref.shape[1] // xs
    for x in range(xs):
        here = slice(x * wide, (x + 1) * wide)
        start = x * 3 * wide
        q_ref[:, here] = (mixed[:, start : start + wide] + bias_ref[0:1, here]).astype(BF16)
        k_ref[:, here] = mixed[:, start + wide : start + 2 * wide].astype(BF16)
        v_ref[:, here] = (
            mixed[:, start + 2 * wide : start + 3 * wide] + bias_ref[1:2, here]
        ).astype(BF16)


def queries(value, weights, order, bias, ys, xs):
    rows = value.shape[0]
    columns = bias.shape[1]
    out = jax.ShapeDtypeStruct((rows, columns), BF16)
    return pl.pallas_call(
        functools.partial(queries_kernel, order, ys, xs),
        grid=(DEPTH,),
        in_specs=[whole(value), by_z(bias.shape[0], columns)] + weight_specs(weights),
        out_specs=[by_z(rows, columns)] * 3,
        out_shape=[out] * 3,
        compiler_params=params(),
        cost_estimate=cost(2 * rows * weight_size(weights), [value, *weights, out, out, out]),
        name="queries",
    )(value, bias, *weights)


def hidden_kernel(order, ys, xs, x_ref, bias_ref, *refs):
    weights, (active_ref, slope_ref) = (refs[:-2], refs[-2:])
    slab = input_slab(weights, order, ys, xs)
    rows = x_ref.shape[0]
    step = min(128, rows)

    def part(i, carry):
        at = pl.ds(pl.multiple_of(i * step, step), step)
        inner = dot(x_ref[at, :], slab) + bias_ref[0:1, :]
        phi = 0.5 * (1.0 + lax.erf(inner * SQRT_HALF))
        active_ref[at, :] = (inner * phi).astype(BF16)
        slope_ref[at, :] = (
            phi + inner * jnp.exp(-0.5 * inner * inner) * ROOT_TWO_PI_INV
        ).astype(BF16)
        return carry

    lax.fori_loop(0, rows // step, part, 0)


def hidden(value, weights, order, bias, ys, xs):
    rows = value.shape[0]
    columns = bias.shape[1]
    out = jax.ShapeDtypeStruct((rows, columns), BF16)
    return pl.pallas_call(
        functools.partial(hidden_kernel, order, ys, xs),
        grid=(DEPTH,),
        in_specs=[whole(value), by_z(bias.shape[0], columns)] + weight_specs(weights),
        out_specs=[by_z(rows, columns)] * 2,
        out_shape=[out] * 2,
        compiler_params=params(),
        cost_estimate=cost(
            2 * rows * weight_size(weights), [value, *weights, out, out], 2 * rows * columns
        ),
        name="hidden",
    )(value, bias, *weights)


def hidden_back_kernel(order, ys, xs, g_ref, slope_ref, *refs):
    weights, (grad_ref, sums_ref) = (refs[:-2], refs[-2:])
    slab = output_slab(weights, order, ys, xs)
    rows = g_ref.shape[0]
    step = min(128, rows)
    sums_ref[...] = jnp.zeros_like(sums_ref)

    def part(i, carry):
        at = pl.ds(pl.multiple_of(i * step, step), step)
        grad = (dot(g_ref[at, :], slab, NT) * slope_ref[at, :].astype(F32)).astype(BF16)
        grad_ref[at, :] = grad
        sums_ref[0:1, :] += jnp.sum(grad.astype(F32), axis=0, keepdims=True)
        return carry

    lax.fori_loop(0, rows // step, part, 0)


def hidden_back(grad, weights, order, slope, ys, xs):
    rows, columns = slope.shape
    out = jax.ShapeDtypeStruct((rows, columns), BF16)
    sums = jax.ShapeDtypeStruct((8, columns), F32)
    return pl.pallas_call(
        functools.partial(hidden_back_kernel, order, ys, xs),
        grid=(DEPTH,),
        in_specs=[whole(grad), by_z(rows, columns)] + weight_specs(weights),
        out_specs=[by_z(rows, columns), by_z(8, columns)],
        out_shape=[out, sums],
        compiler_params=params(),
        cost_estimate=cost(2 * rows * weight_size(weights), [grad, slope, *weights, out]),
        name="hidden_back",
    )(grad, slope, *weights)


def context_back_kernel(order, ys, xs, g_ref, *refs):
    refs[-1][...] = dot(g_ref[...], output_slab(refs[:-1], order, ys, xs), NT).astype(BF16)


def context_back(grad, weights, order, ys, xs):
    rows = grad.shape[0]
    out = jax.ShapeDtypeStruct((rows, HEADS * HEAD_DIM), BF16)
    return pl.pallas_call(
        functools.partial(context_back_kernel, order, ys, xs),
        grid=(DEPTH,),
        in_specs=[whole(grad)] + weight_specs(weights),
        out_specs=by_z(*out.shape),
        out_shape=out,
        compiler_params=params(),
        cost_estimate=cost(2 * rows * weight_size(weights), [grad, *weights, out]),
        name="context_back",
    )(grad, *weights)


def norm_kernel(order, ys, xs, scaled, last, left_ref, base_ref, vec_ref, *refs):
    outs = 4 if last else 3
    weights, results, total = (refs[: -outs - 1], refs[-outs - 1 : -1], refs[-1])
    z = pl.program_id(0)
    product = dot(left_ref[...], output_slab(weights, order, ys, xs))

    @pl.when(z == 0)
    def _():
        total[...] = product

    @pl.when(z > 0)
    def _():
        total[...] += product

    @pl.when(z == DEPTH - 1)
    def _():
        rows = total.shape[0]
        step = min(64, rows)

        def part(i, carry):
            at = pl.ds(pl.multiple_of(i * step, step), step)
            base = base_ref[at, :].astype(F32)
            if scaled:
                base = base * vec_ref[0:1, :] + vec_ref[1:2, :]
            summed = base + (total[at, :] + vec_ref[2:3, :])
            offset = summed - jnp.mean(summed, axis=1, keepdims=True)
            inverse = lax.rsqrt(jnp.mean(offset * offset, axis=1, keepdims=True) + EPSILON)
            normal = offset * inverse
            results[0][at, :] = normal
            results[1][at, :] = jnp.broadcast_to(inverse, (step, 128))
            value = normal * vec_ref[3:4, :] + vec_ref[4:5, :]
            results[2][at, :] = value.astype(BF16)
            if last:
                results[3][at, :] = value
            return carry

        lax.fori_loop(0, rows // step, part, 0)


def norm(left, weights, order, base, vectors, scaled, last, ys, xs):
    rows = left.shape[0]
    width = base.shape[1]
    outs = [
        jax.ShapeDtypeStruct((rows, width), F32),
        jax.ShapeDtypeStruct((rows, 128), F32),
        jax.ShapeDtypeStruct((rows, width), BF16),
    ] + ([jax.ShapeDtypeStruct((rows, width), F32)] if last else [])
    return pl.pallas_call(
        functools.partial(norm_kernel, order, ys, xs, scaled, last),
        grid=(DEPTH,),
        in_specs=[by_z(*left.shape), whole(base), whole(vectors)] + weight_specs(weights),
        out_specs=[whole(o) for o in outs],
        out_shape=outs,
        scratch_shapes=[pltpu.VMEM((rows, width), F32)],
        compiler_params=params(),
        cost_estimate=cost(2 * rows * weight_size(weights), [left, base, *weights, *outs]),
        name="norm",
    )(left, base, vectors, *weights)


def norm_back_rows(upstream, normal, inverse, gain):
    scaled = upstream * gain
    first_mean = jnp.mean(scaled, axis=1, keepdims=True)
    second_mean = jnp.mean(scaled * normal, axis=1, keepdims=True)
    return inverse * (scaled - first_mean - normal * second_mean)


def norm_back_kernel(order, ys, xs, lefts, last, *refs):
    left_refs, rest = (refs[:lefts], refs[lefts:])
    base_ref, rest = (rest[0], rest[1:])
    if not last:
        (normal_ref, inverse_ref, gain_ref), rest = (rest[:3], rest[3:])
    outs = 1 if last else 3
    weights, results, total = (rest[: -outs - 1], rest[-outs - 1 : -1], rest[-1])
    z = pl.program_id(0)
    wide = left_refs[0].shape[1] // xs
    left = jnp.concatenate(
        [ref[:, x * wide : (x + 1) * wide] for x in range(xs) for ref in left_refs], axis=1
    )
    product = dot(left, input_slab(weights, order, ys, xs), NT)

    @pl.when(z == 0)
    def _():
        total[...] = product

    @pl.when(z > 0)
    def _():
        total[...] += product

    @pl.when(z == DEPTH - 1)
    def _():
        if last:
            results[0][...] = base_ref[...] + total[...]
            return
        rows = total.shape[0]
        step = min(64, rows)
        results[2][...] = jnp.zeros_like(results[2])

        def part(i, carry):
            at = pl.ds(pl.multiple_of(i * step, step), step)
            upstream = base_ref[at, :] + total[at, :]
            normal = normal_ref[at, :]
            grad = norm_back_rows(upstream, normal, inverse_ref[at, 0:1], gain_ref[0:1, :])
            low = grad.astype(BF16)
            results[0][at, :] = grad
            results[1][at, :] = low
            results[2][0:1, :] += jnp.sum(upstream, axis=0, keepdims=True)
            results[2][1:2, :] += jnp.sum(upstream * normal, axis=0, keepdims=True)
            results[2][2:3, :] += jnp.sum(low.astype(F32), axis=0, keepdims=True)
            return carry

        lax.fori_loop(0, rows // step, part, 0)


def norm_back(lefts, weights, order, base, saved, ys, xs):
    rows, width = base.shape
    last = saved is None
    outs = [jax.ShapeDtypeStruct((rows, width), F32)]
    if not last:
        outs += [jax.ShapeDtypeStruct((rows, width), BF16), jax.ShapeDtypeStruct((8, width), F32)]
    fixed = [base] + ([] if last else list(saved))
    return pl.pallas_call(
        functools.partial(norm_back_kernel, order, ys, xs, len(lefts), last),
        grid=(DEPTH,),
        in_specs=[by_z(*left.shape) for left in lefts]
        + [whole(v) for v in fixed]
        + weight_specs(weights),
        out_specs=[whole(o) for o in outs],
        out_shape=outs,
        scratch_shapes=[pltpu.VMEM((rows, width), F32)],
        compiler_params=params(),
        cost_estimate=cost(2 * rows * weight_size(weights), [*lefts, *fixed, *weights, *outs]),
        name="norm_back",
    )(*lefts, *fixed, *weights)


def outer_kernel(order, ys, xs, rights, left_ref, other_ref, *refs):
    mine, theirs, rest = (refs[:rights], refs[rights : 2 * rights], refs[2 * rights :])
    outs, turned = (rest[:-1], rest[-1])
    rows = left_ref.shape[0]
    deep = left_ref.shape[1] // (2 * ys)

    @pl.when(pl.program_id(0) == 0)
    def _():
        for y in range(ys):
            turned[y * deep : (y + 1) * deep, :rows] = left_ref[
                :, 2 * y * deep : (2 * y + 1) * deep
            ].T
            turned[y * deep : (y + 1) * deep, rows:] = other_ref[
                :, y * deep : (y + 1) * deep
            ].T

    wide = mine[0].shape[1] // xs
    for x in range(xs):
        here = slice(x * wide, (x + 1) * wide)
        right = jnp.concatenate(
            [
                jnp.concatenate([ref[:, here] for ref in mine], axis=1),
                jnp.concatenate([ref[:, here] for ref in theirs], axis=1),
            ],
            axis=0,
        )
        product = dot(turned[...], right).astype(BF16)
        for y in range(ys):
            block = product[y * deep : (y + 1) * deep]
            if order[1] == "x":
                outs[x][y, 0] = block
            else:
                outs[y][x, 0] = block


def outer(left, other, mine, theirs, order, ys, xs):
    rows, width = left.shape
    deep = width // (2 * ys)
    columns = len(mine) * mine[0].shape[1] // (DEPTH * xs)
    first, second = (xs, ys) if order[1] == "x" else (ys, xs)
    outs = [jax.ShapeDtypeStruct((second, DEPTH, deep, columns), BF16)] * first
    return pl.pallas_call(
        functools.partial(outer_kernel, order, ys, xs, len(mine)),
        grid=(DEPTH,),
        in_specs=[whole(left), whole(other)] + [by_z(*r.shape) for r in [*mine, *theirs]],
        out_specs=[
            pl.BlockSpec((second, 1, deep, columns), lambda z: (0, z, 0, 0)) for _ in outs
        ],
        out_shape=outs,
        scratch_shapes=[pltpu.VMEM((ys * deep, 2 * rows), BF16)],
        compiler_params=params(),
        cost_estimate=cost(
            4 * rows * first * outs[0].size, [left, other, *mine, *theirs, *outs]
        ),
        name="outer",
    )(left, other, *mine, *theirs)


def scores_turned(limits_ref, keys, queries_here):
    pieces = []
    for j, key in enumerate(keys):
        score = dot(key, queries_here, NT) * FACTOR
        place = lax.broadcasted_iota(jnp.int32, score.shape, 0)
        pieces.append(jnp.where(place < limits_ref[j], score, NEGATIVE))
    highest = functools.reduce(
        jnp.maximum, [jnp.max(p, axis=0, keepdims=True) for p in pieces]
    )
    raised = [jnp.exp(p - highest) for p in pieces]
    total = functools.reduce(jnp.add, [jnp.sum(r, axis=0, keepdims=True) for r in raised])
    share = 1.0 / total
    return [r * share for r in raised]


def attend_kernel(parts, limits_ref, q_ref, *refs):
    k_refs, v_refs, out_ref = (refs[:parts], refs[parts : 2 * parts], refs[2 * parts])
    rows = q_ref.shape[0]
    step = min(256, rows)
    for pair in range(q_ref.shape[1] // 128):

        def part(i, carry):
            at = pl.ds(pl.multiple_of(i * step, step), step)
            done = []
            for head in (2 * pair, 2 * pair + 1):
                here = slice(head * HEAD_DIM, (head + 1) * HEAD_DIM)
                probs = scores_turned(
                    limits_ref, [k[:, here] for k in k_refs], q_ref[at, here]
                )
                context = functools.reduce(
                    jnp.add,
                    [
                        dot(v[:, here].T, p.astype(BF16))
                        for v, p in zip(v_refs, probs, strict=True)
                    ],
                )
                done.append(context)
            out_ref[at, pair * 128 : pair * 128 + 128] = (
                jnp.concatenate(done, axis=0).T.astype(BF16)
            )
            return carry

        lax.fori_loop(0, rows // step, part, 0)


def attend(limits, query, keys, values):
    rows, width = query.shape
    elements = rows * rows * len(keys) * HEADS
    return pl.pallas_call(
        functools.partial(attend_kernel, len(keys)),
        grid=(DEPTH,),
        in_specs=[pl.BlockSpec(memory_space=pltpu.SMEM)]
        + [by_z(rows, width)] * (1 + 2 * len(keys)),
        out_specs=by_z(rows, width),
        out_shape=jax.ShapeDtypeStruct((rows, width), BF16),
        compiler_params=params(),
        cost_estimate=cost(4 * 4 * HEAD_DIM * elements, [query, *keys, *values], elements),
        name="attend",
    )(limits, query, *keys, *values)


def attend_back_kernel(parts, limits_ref, q_ref, g_ref, *refs):
    k_refs, v_refs, rest = (refs[:parts], refs[parts : 2 * parts], refs[2 * parts :])
    dq_ref, dk_refs, dv_refs = (rest[0], rest[1 : 1 + parts], rest[1 + parts :])
    for pair in range(q_ref.shape[1] // 128):
        done_q, done_k, done_v = ([], [], [])
        for head in (2 * pair, 2 * pair + 1):
            here = slice(head * HEAD_DIM, (head + 1) * HEAD_DIM)
            query = q_ref[:, here]
            grad = g_ref[:, here]
            probs = scores_turned(limits_ref, [k[:, here] for k in k_refs], query)
            grad_probs = [dot(v[:, here], grad, NT) for v in v_refs]
            weighted = functools.reduce(
                jnp.add,
                [
                    jnp.sum(p * g, axis=0, keepdims=True)
                    for p, g in zip(probs, grad_probs, strict=True)
                ],
            )
            grad_scores = [
                (p * (g - weighted)).astype(BF16)
                for p, g in zip(probs, grad_probs, strict=True)
            ]
            done_v.append([dot(p.astype(BF16), grad) for p in probs])
            done_k.append([dot(s, query) * FACTOR for s in grad_scores])
            done_q.append(
                functools.reduce(
                    jnp.add,
                    [
                        dot(k[:, here].T, s)
                        for k, s in zip(k_refs, grad_scores, strict=True)
                    ],
                )
                * FACTOR
            )
        cols = slice(pair * 128, pair * 128 + 128)
        dq_ref[:, cols] = jnp.concatenate(done_q, axis=0).T.astype(BF16)
        for j in range(parts):
            dk_refs[j][:, cols] = jnp.concatenate([d[j] for d in done_k], axis=1).astype(BF16)
            dv_refs[j][:, cols] = jnp.concatenate([d[j] for d in done_v], axis=1).astype(BF16)


def attend_back(limits, query, grad, keys, values):
    rows, width = query.shape
    parts = len(keys)
    elements = rows * rows * parts * HEADS
    outs = [jax.ShapeDtypeStruct((rows, width), BF16)] * (1 + 2 * parts)
    return pl.pallas_call(
        functools.partial(attend_back_kernel, parts),
        grid=(DEPTH,),
        in_specs=[pl.BlockSpec(memory_space=pltpu.SMEM)] + [by_z(rows, width)] * (2 + 2 * parts),
        out_specs=[by_z(rows, width)] * (1 + 2 * parts),
        out_shape=outs,
        compiler_params=params(),
        cost_estimate=cost(
            10 * 4 * HEAD_DIM * elements, [query, grad, *keys, *values, *outs], elements
        ),
        name="attend_back",
    )(limits, query, grad, *keys, *values)


ORDER = {
    "project": ("y", "x"),
    "combiner": ("x", "y"),
    "expand": ("x", "y"),
    "shrink": ("y", "x"),
}


def shards(
    hidden_in,
    cotangent,
    seq_lengths,
    slot_of,
    project,
    offsets,
    combiner,
    recenter,
    stretch,
    displace,
    expand,
    uplift,
    shrink,
    lowering,
    restretch,
    redisplace,
):
    ys, xs = (lax.axis_size("y"), lax.axis_size("x"))
    y, core, z, x = (lax.axis_index(axis) for axis in ANY_AXES)
    rows, width = hidden_in.shape
    slots_here = seq_lengths.shape[0] // (2 * ys)
    parts = xs
    heads_here = HEADS // (DEPTH * xs)
    paired = parts == 2
    if paired:
        trade = [(a * xs + b, b * xs + a) for a in range(2) for b in range(xs)]
        axis, place, slot_row = ("core", core, 2 * y + x)
    else:
        axis, place, slot_row = ("x", x, 2 * y + core)

    def regroup(value):
        return lax.ppermute(value, ("core", "x"), trade) if paired else value

    def features(value):
        return relative_blocks(value, ("y", "core"))

    slot = slot_row * slots_here + z
    length = jnp.sum(jnp.where(slot_of == slot, seq_lengths, 0))
    limits = jnp.stack([length - ((place - j) % parts) * rows for j in range(parts)])

    def heads_first(block):
        return (
            block.reshape(-1, heads_here, 3, HEAD_DIM).transpose(0, 2, 1, 3).reshape(block.shape)
        )

    weights = []
    for layer in range(LAYERS):
        weights.append(
            {
                "project": gather_weight(heads_first(project[layer]), ORDER["project"]),
                "combiner": gather_weight(combiner[layer], ORDER["combiner"]),
                "expand": gather_weight(expand[layer], ORDER["expand"]),
                "shrink": gather_weight(shrink[layer], ORDER["shrink"]),
            }
        )
    biases = lax.all_gather(
        jnp.concatenate([offsets.reshape(-1), uplift.reshape(-1)]), ("z", "x"), axis=0
    )
    cut = offsets.size
    offsets_full = biases[:, :cut].reshape(-1, LAYERS, heads_here, 2, HEAD_DIM)
    uplift_full = biases[:, cut:].reshape(-1, LAYERS, uplift.shape[1])

    def hidden_order(value):
        return relative_blocks(value, ("z", "x"))

    query_bias = hidden_order(offsets_full[:, :, :, 0].transpose(1, 0, 2, 3).reshape(LAYERS, -1))
    value_bias = hidden_order(offsets_full[:, :, :, 1].transpose(1, 0, 2, 3).reshape(LAYERS, -1))
    inner_bias = hidden_order(uplift_full.transpose(1, 0, 2).reshape(LAYERS, -1))

    start = features(regroup(hidden_in))
    recenter, stretch, displace, lowering, restretch, redisplace = (
        features(v) for v in (recenter, stretch, displace, lowering, restretch, redisplace)
    )
    nothing = jnp.zeros_like(recenter[0])

    def vectors(*items):
        return jnp.stack(list(items) + [nothing] * (8 - len(items)))

    saved = []
    current_low, base, base_gain, base_shift, scaled = (start, start, nothing, nothing, False)
    finished = None
    for layer in range(LAYERS):
        w = weights[layer]
        query, key, value = queries(
            current_low,
            w["project"],
            ORDER["project"],
            vectors(query_bias[layer], value_bias[layer]),
            ys,
            xs,
        )
        keys = spread(key, axis)
        values = spread(value, axis)
        context = attend(limits, query, keys, values)
        normal_one, inverse_one, normed_low = norm(
            context,
            w["combiner"],
            ORDER["combiner"],
            base,
            vectors(base_gain, base_shift, recenter[layer], stretch[layer], displace[layer]),
            scaled,
            False,
            ys,
            xs,
        )
        active, slope = hidden(
            normed_low,
            w["expand"],
            ORDER["expand"],
            jnp.broadcast_to(inner_bias[layer][None], (8, inner_bias.shape[1])),
            ys,
            xs,
        )
        normal_two, inverse_two, next_low, *finished = norm(
            active,
            w["shrink"],
            ORDER["shrink"],
            normal_one,
            vectors(
                stretch[layer], displace[layer], lowering[layer], restretch[layer], redisplace[layer]
            ),
            True,
            layer == LAYERS - 1,
            ys,
            xs,
        )
        saved.append(
            (
                current_low,
                query,
                keys,
                values,
                context,
                normal_one,
                inverse_one,
                normed_low,
                active,
                slope,
                normal_two,
                inverse_two,
            )
        )
        current_low, base, scaled = (next_low, normal_two, True)
        base_gain, base_shift = (restretch[layer], redisplace[layer])
    hidden_out = regroup(features(finished[0]))

    def other_core(value):
        return pull(value, "core", 1)

    def other_features(value):
        return other_core(value.reshape(rows, ys, 2, -1)[:, :, 1].reshape(rows, -1))

    upstream = features(regroup(cotangent))
    _, _, _, _, _, _, _, _, _, _, normal_two, inverse_two = saved[-1]
    grad_two = norm_back_rows(
        upstream, normal_two, inverse_two[:, 0:1], restretch[LAYERS - 1][None]
    )
    grad_two_low = grad_two.astype(BF16)
    sums_two = jnp.stack(
        [
            jnp.sum(upstream, axis=0),
            jnp.sum(upstream * normal_two, axis=0),
            jnp.sum(grad_two_low.astype(F32), axis=0),
        ]
    )
    grads = {name: [] for name in ORDER}
    small = []
    hidden_grad = None
    for layer in reversed(range(LAYERS)):
        w = weights[layer]
        (
            layer_low,
            query,
            keys,
            values,
            context,
            normal_one,
            inverse_one,
            normed_low,
            active,
            slope,
            _,
            _,
        ) = saved[layer]
        grad_inner, sums_inner = hidden_back(
            grad_two_low, w["shrink"], ORDER["shrink"], slope, ys, xs
        )
        grads["shrink"].append(
            scatter_weight(
                outer(
                    grad_two_low,
                    other_features(grad_two_low),
                    [active],
                    [other_core(active)],
                    ORDER["shrink"],
                    ys,
                    xs,
                ),
                ORDER["shrink"],
            ).T
        )
        grads["expand"].append(
            scatter_weight(
                outer(
                    normed_low,
                    other_features(normed_low),
                    [grad_inner],
                    [other_core(grad_inner)],
                    ORDER["expand"],
                    ys,
                    xs,
                ),
                ORDER["expand"],
            )
        )
        grad_one, grad_one_low, sums_one = norm_back(
            [grad_inner],
            w["expand"],
            ORDER["expand"],
            grad_two,
            (normal_one, inverse_one, vectors(stretch[layer])),
            ys,
            xs,
        )
        grads["combiner"].append(
            scatter_weight(
                outer(
                    grad_one_low,
                    other_features(grad_one_low),
                    [context],
                    [other_core(context)],
                    ORDER["combiner"],
                    ys,
                    xs,
                ),
                ORDER["combiner"],
            ).T
        )
        grad_context = context_back(grad_one_low, w["combiner"], ORDER["combiner"], ys, xs)
        grad_query, *pieces = attend_back(limits, query, grad_context, keys, values)
        grad_key = collect(pieces[:parts], axis).astype(BF16)
        grad_value = collect(pieces[parts:], axis).astype(BF16)
        triple = [grad_query, grad_key, grad_value]
        small.append(
            (
                sums_one,
                sums_two,
                sums_inner[0],
                jnp.sum(grad_query.astype(F32), axis=0),
                jnp.sum(grad_value.astype(F32), axis=0),
            )
        )
        lower = None
        if layer > 0:
            lower = (saved[layer - 1][10], saved[layer - 1][11], vectors(restretch[layer - 1]))
        result = norm_back(triple, w["project"], ORDER["project"], grad_one, lower, ys, xs)
        if layer > 0:
            grad_two, grad_two_low, sums_two = result
        else:
            hidden_grad = regroup(features(result[0]))
        turned = scatter_weight(
            outer(
                layer_low,
                other_features(layer_low),
                triple,
                [other_core(t) for t in triple],
                ORDER["project"],
                ys,
                xs,
            ),
            ORDER["project"],
        )
        grads["project"].append(
            turned.reshape(-1, 3, heads_here, HEAD_DIM)
            .transpose(0, 2, 1, 3)
            .reshape(turned.shape)
        )

    def ordered(items):
        return jnp.stack(items[::-1], axis=0)

    def column(flat):
        return flat.reshape(LAYERS, DEPTH * xs, -1)

    totals = []
    for sums_one, sums_two, sums_inner, sums_query, sums_value in small:
        totals.append(
            lax.psum(
                jnp.concatenate(
                    [features(sums_one[s]) for s in range(3)]
                    + [features(sums_two[s]) for s in range(3)]
                    + [hidden_order(sums_inner), hidden_order(sums_query), hidden_order(sums_value)]
                ),
                ANY_AXES,
            )
        )
    total = ordered(totals)
    norms = total[:, : 6 * width].reshape(LAYERS, 6, width)
    rest = total[:, 6 * width :]
    units = sums_inner.shape[0]
    here = z * xs + x

    def own(flat):
        return lax.dynamic_index_in_dim(column(flat), here, 1, keepdims=False)

    uplift_grad = own(rest[:, :units])
    query_grad = own(rest[:, units : units + width]).reshape(LAYERS, heads_here, HEAD_DIM)
    value_grad = own(rest[:, units + width :]).reshape(LAYERS, heads_here, HEAD_DIM)
    offsets_grad = jnp.stack([query_grad, value_grad], axis=2).reshape(LAYERS, -1)
    return (
        hidden_out,
        hidden_grad,
        ordered(grads["project"]),
        offsets_grad,
        ordered(grads["combiner"]),
        norms[:, 2],
        norms[:, 1],
        norms[:, 0],
        ordered(grads["expand"]),
        uplift_grad,
        ordered(grads["shrink"]),
        norms[:, 5],
        norms[:, 4],
        norms[:, 3],
    )


def solution(mesh):
    rows, columns = (mesh.shape["row"], mesh.shape["col"])
    fine = Mesh(mesh.devices.reshape(rows // 2, 2, DEPTH, columns // DEPTH), ANY_AXES)
    row, col = (("y", "core"), ("z", "x"))
    in_specs = (
        P(ANY_AXES, None),
        P(ANY_AXES, None),
        P(),
        P(),
        P(None, row, col),
        P(None, col),
        P(None, col, row),
        P(),
        P(),
        P(),
        P(None, row, col),
        P(None, col),
        P(None, col, row),
        P(),
        P(),
        P(),
    )
    out_specs = (
        P(ANY_AXES, None),
        P(ANY_AXES, None),
        P(None, row, col),
        P(None, col),
        P(None, col, row),
        P(),
        P(),
        P(),
        P(None, row, col),
        P(None, col),
        P(None, col, row),
        P(),
        P(),
        P(),
    )
    return jax.shard_map(shards, mesh=fine, in_specs=in_specs, out_specs=out_specs, check_vma=False)
```

```python
import functools
import math

import jax
import jax.numpy as jnp
from jax import lax
from jax.experimental import pallas as pl
from jax.experimental.pallas import tpu as pltpu
from jax.sharding import Mesh, PartitionSpec as P

HEADS = 16
HEAD_DIM = 64
LAYERS = 2
DEPTH = 4

EPSILON = 1e-12
NEGATIVE = -1e30
SQRT_HALF = 0.7071067811865476
ROOT_TWO_PI_INV = 0.3989422804014327
FACTOR = 1.0 / math.sqrt(HEAD_DIM)
VMEM = 52 * 1024 * 1024
F32 = jnp.float32
BF16 = jnp.bfloat16
NT = (((1,), (1,)), ((), ()))
NN = (((1,), (0,)), ((), ()))
ANY_AXES = ("y", "core", "z", "x")


def dot(left, right, dims=NN):
    return lax.dot_general(left, right, dims, preferred_element_type=F32)


def pull(value, axis, step):
    size = lax.axis_size(axis)
    return lax.ppermute(value, axis, [(i, (i + step) % size) for i in range(size)])


def push(value, axis, step):
    size = lax.axis_size(axis)
    return lax.ppermute(value, axis, [(i, (i - step) % size) for i in range(size)])


def spread(value, axis):
    return [value] + [pull(value, axis, s) for s in range(1, lax.axis_size(axis))]


class Gather:
    def __init__(self, block, order):
        self.order = order
        self.stage = 0
        self.parts = spread(block, "z")

    def advance(self):
        self.stage += 1
        if self.stage <= 2:
            value = jnp.stack(self.parts)
            self.parts = spread(value, self.order[self.stage - 1])
            return [value]
        if self.stage == 3:
            own = self.parts
            self.parts = own + [pull(piece, "core", 1) for piece in own]
            return own[1:]
        return []

    def pieces(self):
        while self.stage < 4:
            self.advance()
        return self.parts


class Scatter:
    def __init__(self, pieces, order):
        self.axes = (order[1], order[0], "z")
        self.stage = 0
        self.own = pieces[0]
        self.parts = send(pieces, self.axes[0])

    def advance(self):
        total = functools.reduce(jnp.add, [p.astype(F32) for p in [self.own] + self.parts])
        self.stage += 1
        if self.stage == 3:
            self.result = total
            return [total]
        total = total.astype(BF16)
        pieces = [total[s] for s in range(total.shape[0])]
        self.own = pieces[0]
        self.parts = send(pieces, self.axes[self.stage])
        return [total]

    def finish(self):
        while self.stage < 3:
            self.advance()
        return self.result


def send(pieces, axis):
    return [push(pieces[s], axis, s) for s in range(1, lax.axis_size(axis))]


def add_over(value, axes):
    for axis in axes:
        value = functools.reduce(jnp.add, spread(value, axis))
    return value


def relative_blocks(value, axes):
    sizes = [lax.axis_size(axis) for axis in axes]
    count = math.prod(sizes)
    width = value.shape[-1] // count
    parts = []
    for place in range(count):
        low = place % sizes[1]
        high = place // sizes[1]
        source = ((lax.axis_index(axes[0]) - high) % sizes[0]) * sizes[1] + (
            lax.axis_index(axes[1]) - low
        ) % sizes[1]
        parts.append(lax.dynamic_slice_in_dim(value, source * width, width, value.ndim - 1))
    return jnp.concatenate(parts, axis=-1)


def tile(refs, order, core, y, x):
    half = len(refs) // 2
    if order[1] == "x":
        return refs[core * half + x][y, 0]
    return refs[core * half + y][x, 0]


def slab(refs, order, ys, xs, span):
    return jnp.concatenate(
        [
            jnp.concatenate(
                [tile(refs, order, core, y, x)[:, span[0] : span[1]] for x in range(xs)], axis=1
            )
            for y in range(ys)
            for core in range(2)
        ],
        axis=0,
    )


def weight_specs(weights):
    return [
        pl.BlockSpec((w.shape[0], 1, w.shape[2], w.shape[3]), lambda z: (0, z, 0, 0))
        for w in weights
    ]


def whole(value):
    return pl.BlockSpec(value.shape, lambda z: (0,) * len(value.shape))


def by_z(rows, columns):
    return pl.BlockSpec((rows, columns // DEPTH), lambda z: (0, z))


ORDERS = (
    (("y", "x"), ("x", "y"), ("y", "x")),
    (("x", "y"), ("y", "x"), ("x", "y")),
)
COST = 1000


def forward_waits(a0, e0, s0, a1, e1, s1):
    return (
        {
            "queries": (e0, s0),
            "attend": (s0,),
            "norm": (e0, a1),
            "hidden": (s0, e1),
            "norm_two": (a1, s1),
        },
        {"queries": (e1,), "attend": (s1,), "norm": (e1,), "hidden": (s1,), "norm_two": ()},
    )


def call(kernel, name, ins, outs, scratch=(), tokens=()):
    skip = len(tokens)

    def body(*refs):
        kernel(*refs[skip:])

    return list(pl.pallas_call(
        body,
        grid=(DEPTH,),
        in_specs=[pl.BlockSpec(memory_space=pl.ANY)] * skip + [spec for _, spec in ins],
        out_specs=[spec for _, spec in outs],
        out_shape=[shape for shape, _ in outs],
        scratch_shapes=list(scratch),
        compiler_params=pltpu.CompilerParams(
            vmem_limit_bytes=VMEM, dimension_semantics=("arbitrary",)
        ),
        cost_estimate=pl.CostEstimate(flops=COST, bytes_accessed=COST, transcendentals=0),
        name=name,
    )(*tokens, *[array for array, _ in ins]))


def shape(rows, columns, dtype=BF16):
    return jax.ShapeDtypeStruct((rows, columns), dtype)


def kept(array):
    return (array, whole(array))


def split(array):
    return (array, by_z(*array.shape))


def weighted(weights):
    return list(zip(weights, weight_specs(weights), strict=True))


def queries(value, weights, order, bias, ys, xs, tokens):
    rows, columns = (value.shape[0], bias.shape[1])
    wide = columns // (DEPTH * xs)

    def kernel(x_ref, bias_ref, *refs):
        q_ref, k_ref, v_ref = refs[-3:]
        mixed = dot(x_ref[...], slab(refs[:-3], order, ys, xs, (0, 3 * wide)))
        for x in range(xs):
            here = slice(x * wide, (x + 1) * wide)
            start = x * 3 * wide
            q_ref[:, here] = (mixed[:, start : start + wide] + bias_ref[0:1, here]).astype(BF16)
            k_ref[:, here] = mixed[:, start + wide : start + 2 * wide].astype(BF16)
            v_ref[:, here] = (
                mixed[:, start + 2 * wide : start + 3 * wide] + bias_ref[1:2, here]
            ).astype(BF16)

    return call(
        kernel,
        "queries",
        [kept(value), split(bias), *weighted(weights)],
        [split(shape(rows, columns))] * 3,
        tokens=tokens,
    )


def hidden(value, weights, order, bias, ys, xs, tokens):
    rows, columns = (value.shape[0], bias.shape[1])
    wide = columns // DEPTH
    step = min(64, rows)

    def kernel(x_ref, bias_ref, *refs):
        active_ref, slope_ref, inner_ref = refs[-3:]
        inner_ref[...] = dot(x_ref[...], slab(refs[:-3], order, ys, xs, (0, wide // xs)))

        def part(i, carry):
            at = pl.ds(pl.multiple_of(i * step, step), step)
            inner = inner_ref[at, :] + bias_ref[0:1, :]
            phi = 0.5 * (1.0 + lax.erf(inner * SQRT_HALF))
            active_ref[at, :] = (inner * phi).astype(BF16)
            slope_ref[at, :] = (
                phi + inner * jnp.exp(-0.5 * inner * inner) * ROOT_TWO_PI_INV
            ).astype(BF16)
            return carry

        lax.fori_loop(0, rows // step, part, 0)

    return call(
        kernel,
        "hidden",
        [kept(value), split(bias), *weighted(weights)],
        [split(shape(rows, columns))] * 2,
        [pltpu.VMEM((rows, wide), F32)],
        tokens,
    )


def hidden_back(grad, weights, order, slope, ys, xs, tokens):
    rows, columns = slope.shape
    wide = columns // DEPTH
    step = min(64, rows)

    def kernel(g_ref, slope_ref, *refs):
        grad_ref, sums_ref, back_ref = refs[-3:]
        back_ref[...] = dot(g_ref[...], slab(refs[:-3], order, ys, xs, (0, wide // xs)))
        sums_ref[...] = jnp.zeros_like(sums_ref)

        def part(i, carry):
            at = pl.ds(pl.multiple_of(i * step, step), step)
            value = (back_ref[at, :] * slope_ref[at, :].astype(F32)).astype(BF16)
            grad_ref[at, :] = value
            sums_ref[0:1, :] += jnp.sum(value.astype(F32), axis=0, keepdims=True)
            return carry

        lax.fori_loop(0, rows // step, part, 0)

    return call(
        kernel,
        "hidden_back",
        [kept(grad), split(slope), *weighted(weights)],
        [split(shape(rows, columns)), split(shape(8, columns, F32))],
        [pltpu.VMEM((rows, wide), F32)],
        tokens,
    )


def context_back(grad, weights, order, ys, xs, tokens):
    rows = grad.shape[0]
    wide = HEADS * HEAD_DIM // (DEPTH * xs)

    def kernel(g_ref, *refs):
        value = dot(g_ref[...], slab(refs[:-1], order, ys, xs, (3 * wide, 4 * wide)))
        refs[-1][...] = value.astype(BF16)

    return call(
        kernel,
        "context_back",
        [kept(grad), *weighted(weights)],
        [split(shape(rows, HEADS * HEAD_DIM))],
        tokens=tokens,
    )[0]


def gathered(total, product):
    z = pl.program_id(0)

    @pl.when(z == 0)
    def _():
        total[...] = product

    @pl.when(z > 0)
    def _():
        total[...] += product


def other_half(value, half_ref, at, ys):
    deep = value.shape[1] // (2 * ys)
    for y in range(ys):
        half_ref[at, y * deep : (y + 1) * deep] = value[:, (2 * y + 1) * deep : (2 * y + 2) * deep]


def norm(left, weights, order, span, base, vectors, scaled, last, ys, xs, tokens):
    rows, width = base.shape
    step = min(64, rows)

    def kernel(left_ref, base_ref, vec_ref, *refs):
        outs = 5 if last else 4
        results, total = (refs[-outs - 1 : -1], refs[-1])
        gathered(
            total, dot(left_ref[...], slab(refs[: -outs - 1], order, ys, xs, span), NT)
        )

        @pl.when(pl.program_id(0) == DEPTH - 1)
        def _():
            def part(i, carry):
                at = pl.ds(pl.multiple_of(i * step, step), step)
                base_here = base_ref[at, :].astype(F32)
                if scaled:
                    base_here = base_here * vec_ref[0:1, :] + vec_ref[1:2, :]
                summed = base_here + (total[at, :] + vec_ref[2:3, :])
                offset = summed - jnp.mean(summed, axis=1, keepdims=True)
                inverse = lax.rsqrt(jnp.mean(offset * offset, axis=1, keepdims=True) + EPSILON)
                normal = offset * inverse
                results[0][at, :] = normal
                results[1][at, :] = jnp.broadcast_to(inverse, (step, 128))
                value = normal * vec_ref[3:4, :] + vec_ref[4:5, :]
                low = value.astype(BF16)
                results[2][at, :] = low
                other_half(low, results[3], at, ys)
                if last:
                    results[4][at, :] = value
                return carry

            lax.fori_loop(0, rows // step, part, 0)

    outs = [
        shape(rows, width, F32),
        shape(rows, 128, F32),
        shape(rows, width),
        shape(rows, width // 2),
    ] + ([shape(rows, width, F32)] if last else [])
    return call(
        kernel,
        "norm",
        [split(left), kept(base), kept(vectors), *weighted(weights)],
        [kept(o) for o in outs],
        [pltpu.VMEM((rows, width), F32)],
        tokens,
    )


def norm_back(lefts, weights, order, span, base, saved, ys, xs, tokens):
    rows, width = base.shape
    step = min(64, rows)
    last = saved is None
    outs = [shape(rows, width, F32)]
    if not last:
        outs += [shape(rows, width), shape(rows, width // 2), shape(8, width, F32)]

    def kernel(*refs):
        left_refs, refs = (refs[: len(lefts)], refs[len(lefts) :])
        base_ref, refs = (refs[0], refs[1:])
        if not last:
            (normal_ref, inverse_ref, gain_ref), refs = (refs[:3], refs[3:])
        results, total = (refs[-len(outs) - 1 : -1], refs[-1])
        if lefts:
            wide = left_refs[0].shape[1] // xs
            left = jnp.concatenate(
                [ref[:, x * wide : (x + 1) * wide] for x in range(xs) for ref in left_refs],
                axis=1,
            )
            tiles = refs[: -len(outs) - 1]
            gathered(total, dot(left, slab(tiles, order, ys, xs, span), NT))

        @pl.when(pl.program_id(0) == DEPTH - 1)
        def _():
            if last:
                results[0][...] = base_ref[...] + total[...]
                return
            results[3][...] = jnp.zeros_like(results[3])

            def part(i, carry):
                at = pl.ds(pl.multiple_of(i * step, step), step)
                upstream = base_ref[at, :]
                if lefts:
                    upstream = upstream + total[at, :]
                normal = normal_ref[at, :]
                scaled = upstream * gain_ref[0:1, :]
                first_mean = jnp.mean(scaled, axis=1, keepdims=True)
                second_mean = jnp.mean(scaled * normal, axis=1, keepdims=True)
                grad = inverse_ref[at, 0:1] * (scaled - first_mean - normal * second_mean)
                low = grad.astype(BF16)
                results[0][at, :] = grad
                results[1][at, :] = low
                other_half(low, results[2], at, ys)
                results[3][0:1, :] += jnp.sum(upstream, axis=0, keepdims=True)
                results[3][1:2, :] += jnp.sum(upstream * normal, axis=0, keepdims=True)
                results[3][2:3, :] += jnp.sum(low.astype(F32), axis=0, keepdims=True)
                return carry

            lax.fori_loop(0, rows // step, part, 0)

    fixed = [base] + ([] if last else list(saved))
    return call(
        kernel,
        "norm_back",
        [split(v) for v in lefts] + [kept(v) for v in fixed] + weighted(weights),
        [kept(o) for o in outs],
        [pltpu.VMEM((rows, width), F32)],
        tokens,
    )


def outer(groups, order, ys, xs, tokens=()):
    rows, width = groups[0][0].shape
    deep = width // (2 * ys)
    widths = [sum(r.shape[1] for r in mine) // (DEPTH * xs) for _, _, mine, _ in groups]
    first, second = (xs, ys) if order[1] == "x" else (ys, xs)
    counts = [2 + 2 * len(mine) for _, _, mine, _ in groups]

    def kernel(*refs):
        inputs, refs = (refs[: sum(counts)], refs[sum(counts) :])
        outs, turned = (refs[:first], refs[first:])
        column = 0
        for g, (_, _, group, _) in enumerate(groups):
            rights = len(group)
            left_ref, other_ref = inputs[:2]
            mine, theirs = (inputs[2 : 2 + rights], inputs[2 + rights : 2 + 2 * rights])
            inputs = inputs[counts[g] :]
            both = turned[g]

            @pl.when(pl.program_id(0) == 0)
            def _(left_ref=left_ref, other_ref=other_ref, both=both):
                for y in range(ys):
                    here = slice(y * deep, (y + 1) * deep)
                    both[here, :rows] = left_ref[:, 2 * y * deep : (2 * y + 1) * deep].T
                    both[here, rows:] = other_ref[:, here].T

            wide = mine[0].shape[1] // xs
            for x in range(xs):
                here = slice(x * wide, (x + 1) * wide)
                right = jnp.concatenate(
                    [
                        jnp.concatenate([ref[:, here] for ref in mine], axis=1),
                        jnp.concatenate([ref[:, here] for ref in theirs], axis=1),
                    ],
                    axis=0,
                )
                product = dot(both[...], right).astype(BF16)
                span = slice(column, column + widths[g])
                for y in range(ys):
                    block = product[y * deep : (y + 1) * deep]
                    if order[1] == "x":
                        outs[x][y, 0, :, span] = block
                    else:
                        outs[y][x, 0, :, span] = block
            column += widths[g]

    spec = pl.BlockSpec((second, 1, deep, sum(widths)), lambda z: (0, z, 0, 0))
    out = jax.ShapeDtypeStruct((second, DEPTH, deep, sum(widths)), BF16)
    ins = []
    for left, other, mine, theirs in groups:
        ins += [kept(left), kept(other)] + [split(r) for r in [*mine, *theirs]]
    return call(
        kernel,
        "outer",
        ins,
        [(out, spec)] * first,
        [pltpu.VMEM((ys * deep, 2 * rows), BF16)] * len(groups),
        tokens,
    )


def probabilities(limits_ref, keys, query):
    pieces = []
    for j, key in enumerate(keys):
        score = dot(key, query, NT) * FACTOR
        place = lax.broadcasted_iota(jnp.int32, score.shape, 0)
        pieces.append(jnp.where(place < limits_ref[j], score, NEGATIVE))
    highest = functools.reduce(
        jnp.maximum, [jnp.max(p, axis=0, keepdims=True) for p in pieces]
    )
    raised = [jnp.exp(p - highest) for p in pieces]
    total = functools.reduce(jnp.add, [jnp.sum(r, axis=0, keepdims=True) for r in raised])
    return raised, 1.0 / total


def total_of(items):
    return functools.reduce(jnp.add, items)


def attend(limits, query, keys, values, tokens):
    rows, _ = query.shape
    parts = len(keys)
    step = min(256, rows)

    def kernel(limits_ref, q_ref, *refs):
        k_refs, v_refs, out_ref = (refs[:parts], refs[parts : 2 * parts], refs[2 * parts])
        for pair in range(q_ref.shape[1] // 128):

            def part(i, carry, pair=pair):
                at = pl.ds(pl.multiple_of(i * step, step), step)
                done = []
                for head in (2 * pair, 2 * pair + 1):
                    here = slice(head * HEAD_DIM, (head + 1) * HEAD_DIM)
                    raised, share = probabilities(
                        limits_ref, [k[:, here] for k in k_refs], q_ref[at, here]
                    )
                    done.append(
                        total_of(
                            dot(v[:, here].T, (r * share).astype(BF16))
                            for v, r in zip(v_refs, raised, strict=True)
                        )
                    )
                out_ref[at, pair * 128 : pair * 128 + 128] = (
                    jnp.concatenate(done, axis=0).T.astype(BF16)
                )
                return carry

            lax.fori_loop(0, rows // step, part, 0)

    return call(
        kernel,
        "attend",
        [(limits, pl.BlockSpec(memory_space=pltpu.SMEM))]
        + [split(v) for v in [query, *keys, *values]],
        [split(query)],
        tokens=tokens,
    )[0]


def attend_back(limits, query, grad, keys, values, tokens):
    parts = len(keys)

    def kernel(limits_ref, q_ref, g_ref, *refs):
        k_refs, v_refs, refs = (refs[:parts], refs[parts : 2 * parts], refs[2 * parts :])
        dq_ref, dk_refs, dv_refs = (refs[0], refs[1 : 1 + parts], refs[1 + parts : 1 + 2 * parts])
        sums_ref = refs[-1]
        sums_ref[...] = jnp.zeros_like(sums_ref)
        for pair in range(q_ref.shape[1] // 128):
            done_q, done_k, done_v = ([], [], [])
            for head in (2 * pair, 2 * pair + 1):
                here = slice(head * HEAD_DIM, (head + 1) * HEAD_DIM)
                query_here = q_ref[:, here]
                grad_here = g_ref[:, here]
                raised, share = probabilities(limits_ref, [k[:, here] for k in k_refs], query_here)
                probs = [r * share for r in raised]
                grad_probs = [dot(v[:, here], grad_here, NT) for v in v_refs]
                mean = total_of(
                    jnp.sum(p * g, axis=0, keepdims=True)
                    for p, g in zip(probs, grad_probs, strict=True)
                )
                grad_scores = [
                    (p * (g - mean)).astype(BF16) for p, g in zip(probs, grad_probs, strict=True)
                ]
                done_v.append([dot(p.astype(BF16), grad_here) for p in probs])
                done_k.append([dot(s, query_here) * FACTOR for s in grad_scores])
                done_q.append(
                    total_of(
                        dot(k[:, here].T, s) for k, s in zip(k_refs, grad_scores, strict=True)
                    )
                    * FACTOR
                )
            cols = slice(pair * 128, pair * 128 + 128)
            low = jnp.concatenate(done_q, axis=0).T.astype(BF16)
            dq_ref[:, cols] = low
            sums_ref[0:1, cols] = jnp.sum(low.astype(F32), axis=0, keepdims=True)
            for j in range(parts):
                dk_refs[j][:, cols] = jnp.concatenate([d[j] for d in done_k], axis=1).astype(BF16)
                grad_value = jnp.concatenate([d[j] for d in done_v], axis=1)
                dv_refs[j][:, cols] = grad_value.astype(BF16)
                sums_ref[1:2, cols] += jnp.sum(grad_value, axis=0, keepdims=True)

    return call(
        kernel,
        "attend_back",
        [(limits, pl.BlockSpec(memory_space=pltpu.SMEM))]
        + [split(v) for v in [query, grad, *keys, *values]],
        [split(query)] * (1 + 2 * parts) + [split(shape(8, query.shape[1], F32))],
        tokens=tokens,
    )


def shards(
    hidden_in,
    cotangent,
    seq_lengths,
    slot_of,
    project,
    offsets,
    combiner,
    recenter,
    stretch,
    displace,
    expand,
    uplift,
    shrink,
    lowering,
    restretch,
    redisplace,
):
    ys, xs = (lax.axis_size("y"), lax.axis_size("x"))
    y, core, z, x = (lax.axis_index(axis) for axis in ANY_AXES)
    rows, width = hidden_in.shape
    slots_here = seq_lengths.shape[0] // (2 * ys)
    parts = xs
    heads_here = HEADS // (DEPTH * xs)
    wide = heads_here * HEAD_DIM
    paired = parts == 2
    if paired:
        trade = [(a * xs + b, b * xs + a) for a in range(2) for b in range(xs) if a != b]
        axis, place, slot_row = ("core", core, 2 * y + x)
    else:
        axis, place, slot_row = ("x", x, 2 * y + core)

    def regroup(value):
        if not paired:
            return value
        return jnp.where(core == x, value, lax.ppermute(value, ("core", "x"), trade))

    def features(value):
        return relative_blocks(value, ("y", "core"))

    slot = slot_row * slots_here + z
    length = jnp.sum(jnp.where(slot_of == slot, seq_lengths, 0))
    limits = jnp.stack([length - ((place - j) % parts) * rows for j in range(parts)])

    def heads_first(block):
        return (
            block.reshape(-1, heads_here, 3, HEAD_DIM).transpose(0, 2, 1, 3).reshape(block.shape)
        )

    start = features(regroup(hidden_in))
    blocks = []
    for layer in range(LAYERS):
        blocks.append(
            (
                jnp.concatenate([heads_first(project[layer]), combiner[layer].T], axis=1),
                expand[layer],
                shrink[layer].T,
            )
        )
    span_project, span_combiner = ((0, 3 * wide), (3 * wide, 4 * wide))
    span_hidden = (0, expand.shape[2])
    gathers = [
        [Gather(b, order) for b, order in zip(blocks[layer], ORDERS[layer], strict=True)]
        for layer in range(LAYERS)
    ]
    biases = jnp.concatenate([offsets.reshape(-1), uplift.reshape(-1)])
    biases = jnp.stack(spread(jnp.stack(spread(biases, "x")), "z"))
    biases = biases.reshape(DEPTH * xs, -1)
    cut = offsets.size
    offsets_full = biases[:, :cut].reshape(-1, LAYERS, heads_here, 2, HEAD_DIM)
    uplift_full = biases[:, cut:].reshape(-1, LAYERS, uplift.shape[1])
    query_bias = offsets_full[:, :, :, 0].transpose(1, 0, 2, 3).reshape(LAYERS, -1)
    value_bias = offsets_full[:, :, :, 1].transpose(1, 0, 2, 3).reshape(LAYERS, -1)
    inner_bias = uplift_full.transpose(1, 0, 2).reshape(LAYERS, -1)

    recenter, stretch, displace, lowering, restretch, redisplace = features(
        jnp.stack([recenter, stretch, displace, lowering, restretch, redisplace])
    )
    nothing = jnp.zeros_like(recenter[0])

    def vectors(*items):
        return jnp.stack(list(items) + [nothing] * (8 - len(items)))

    def other_core(value):
        return pull(value, "core", 1)

    def advance(*flows):
        return sum([flow.advance() for flow in flows], [])

    half = start.reshape(rows, ys, 2, -1)[:, :, 1].reshape(rows, -1)
    saved = []
    current_low, base, base_gain, base_shift, scaled = (start, start, nothing, nothing, False)
    finished = None
    (a0, e0, s0), (a1, e1, s1) = gathers
    waits = forward_waits(a0, e0, s0, a1, e1, s1)
    for layer in range(LAYERS):
        order_a, order_e, order_s = ORDERS[layer]
        gather_a, gather_e, gather_s = gathers[layer]
        weights_a = gather_a.pieces()
        query, key, value = queries(
            current_low,
            weights_a,
            order_a,
            vectors(query_bias[layer], value_bias[layer]),
            ys,
            xs,
            advance(*waits[layer]["queries"]),
        )
        keys = spread(key, axis)
        values = spread(value, axis)
        context = attend(limits, query, keys, values, advance(*waits[layer]["attend"]))
        normal_one, inverse_one, normed_low, normed_half = norm(
            context,
            weights_a,
            order_a,
            span_combiner,
            base,
            vectors(base_gain, base_shift, recenter[layer], stretch[layer], displace[layer]),
            scaled,
            False,
            ys,
            xs,
            advance(*waits[layer]["norm"]),
        )
        weights_e = gather_e.pieces()
        active, slope = hidden(
            normed_low,
            weights_e,
            order_e,
            jnp.broadcast_to(inner_bias[layer][None], (8, inner_bias.shape[1])),
            ys,
            xs,
            advance(*waits[layer]["hidden"]),
        )
        weights_s = gather_s.pieces()
        normal_two, inverse_two, next_low, next_half, *finished = norm(
            active,
            weights_s,
            order_s,
            span_hidden,
            normal_one,
            vectors(
                stretch[layer], displace[layer], lowering[layer], restretch[layer], redisplace[layer]
            ),
            True,
            layer == LAYERS - 1,
            ys,
            xs,
            advance(*waits[layer]["norm_two"]),
        )
        saved.append(
            {
                "low": current_low,
                "low_half": other_core(half),
                "query": query,
                "keys": keys,
                "values": values,
                "context": context,
                "context_other": other_core(context),
                "one": (normal_one, inverse_one),
                "normed": normed_low,
                "normed_half": other_core(normed_half),
                "active": active,
                "active_other": other_core(active),
                "slope": slope,
                "two": (normal_two, inverse_two, vectors(restretch[layer])),
                "weights": (weights_a, weights_e, weights_s),
            }
        )
        current_low, half, base, scaled = (next_low, next_half, normal_two, True)
        base_gain, base_shift = (restretch[layer], redisplace[layer])
    hidden_out = regroup(features(finished[0]))

    upstream = features(regroup(cotangent))
    grad_two, low_two, half_two, sums_two = norm_back(
        [], [], None, None, upstream, saved[-1]["two"], ys, xs, []
    )
    flows = {}
    small = []
    hidden_grad = None

    def turn(*names):
        return advance(*[flows[name] for name in names if name in flows])

    for layer in reversed(range(LAYERS)):
        kept_here = saved[layer]
        weights_a, weights_e, weights_s = kept_here["weights"]
        order_a, order_e, order_s = ORDERS[layer]
        above = layer + 1
        grad_inner, sums_inner = hidden_back(
            low_two,
            weights_s,
            order_s,
            kept_here["slope"],
            ys,
            xs,
            turn(("s", above)),
        )
        out_s = outer(
            [(low_two, other_core(half_two), [kept_here["active"]], [kept_here["active_other"]])],
            order_s,
            ys,
            xs,
            turn(("e", above)),
        )
        flows["s", layer] = Scatter(out_s, order_s)
        grad_one, low_one, half_one, sums_one = norm_back(
            [grad_inner],
            weights_e,
            order_e,
            span_hidden,
            grad_two,
            (*kept_here["one"], vectors(stretch[layer])),
            ys,
            xs,
            out_s + turn(("p", above)),
        )
        out_e = outer(
            [
                (
                    kept_here["normed"],
                    kept_here["normed_half"],
                    [grad_inner],
                    [other_core(grad_inner)],
                ),
                (
                    low_one,
                    other_core(half_one),
                    [kept_here["context"]],
                    [kept_here["context_other"]],
                ),
            ],
            order_e,
            ys,
            xs,
            turn(("s", above)),
        )
        flows["e", layer] = Scatter(out_e, order_e)
        grad_context = context_back(low_one, weights_a, order_a, ys, xs, out_e)
        grad_query, *pieces, sums_attend = attend_back(
            limits,
            kept_here["query"],
            grad_context,
            kept_here["keys"],
            kept_here["values"],
            turn(("e", above), ("p", above)),
        )
        grad_key = total_of(
            p.astype(F32) for p in [pieces[0]] + send(pieces[:parts], axis)
        ).astype(BF16)
        grad_value = total_of(
            p.astype(F32) for p in [pieces[parts]] + send(pieces[parts:], axis)
        ).astype(BF16)
        triple = [grad_query, grad_key, grad_value]
        small.append((sums_one, sums_two, sums_inner, sums_attend))
        result = norm_back(
            triple,
            weights_a,
            order_a,
            span_project,
            grad_one,
            saved[layer - 1]["two"] if layer > 0 else None,
            ys,
            xs,
            turn(("s", layer), ("p", above)),
        )
        if layer > 0:
            grad_two, low_two, half_two, sums_two = result
        else:
            hidden_grad = regroup(features(result[0]))
        out_p = outer(
            [
                (
                    kept_here["low"],
                    kept_here["low_half"],
                    triple,
                    [other_core(t) for t in triple],
                )
            ],
            order_a,
            ys,
            xs,
            turn(("e", layer)),
        )
        flows["p", layer] = Scatter(out_p, order_a)

    def ordered(items):
        return jnp.stack(items, axis=0)

    def hidden_order(value):
        return relative_blocks(value, ("z", "x"))

    totals = []
    for sums_one, sums_two, sums_inner, sums_attend in small[::-1]:
        totals.append(
            add_over(
                jnp.concatenate(
                    [features(sums_one[:3]).reshape(-1), features(sums_two[:3]).reshape(-1)]
                    + [hidden_order(sums_inner[0]), hidden_order(sums_attend[:2]).reshape(-1)]
                ),
                ANY_AXES,
            )
        )
    total = ordered(totals)
    norms = total[:, : 6 * width].reshape(LAYERS, 6, width)
    rest = total[:, 6 * width :]
    units = rest.shape[1] - 2 * width
    here = z * xs + x

    def own(flat):
        columns = flat.reshape(LAYERS, DEPTH * xs, -1)
        return lax.dynamic_index_in_dim(columns, here, 1, keepdims=False)

    uplift_grad = own(rest[:, :units])
    query_grad = own(rest[:, units : units + width]).reshape(LAYERS, heads_here, HEAD_DIM)
    value_grad = own(rest[:, units + width :]).reshape(LAYERS, heads_here, HEAD_DIM)
    offsets_grad = jnp.stack([query_grad, value_grad], axis=2).reshape(LAYERS, -1)

    def heads_last(block):
        return (
            block.reshape(-1, 3, heads_here, HEAD_DIM).transpose(0, 2, 1, 3).reshape(block.shape)
        )

    shrink_grad = ordered([flows["s", layer].finish().T for layer in range(LAYERS)])
    wide_grads = [flows["e", layer].finish() for layer in range(LAYERS)]
    expand_grad = ordered([m[:, : span_hidden[1]] for m in wide_grads])
    combiner_grad = ordered([m[:, span_hidden[1] :].T for m in wide_grads])
    project_grad = ordered([heads_last(flows["p", layer].finish()) for layer in range(LAYERS)])
    return (
        hidden_out,
        hidden_grad,
        project_grad,
        offsets_grad,
        combiner_grad,
        norms[:, 2],
        norms[:, 1],
        norms[:, 0],
        expand_grad,
        uplift_grad,
        shrink_grad,
        norms[:, 5],
        norms[:, 4],
        norms[:, 3],
    )


def solution(mesh):
    rows, columns = (mesh.shape["row"], mesh.shape["col"])
    fine = Mesh(mesh.devices.reshape(rows // 2, 2, DEPTH, columns // DEPTH), ANY_AXES)
    row, col = (("y", "core"), ("z", "x"))
    in_specs = (
        P(ANY_AXES, None),
        P(ANY_AXES, None),
        P(),
        P(),
        P(None, row, col),
        P(None, col),
        P(None, col, row),
        P(),
        P(),
        P(),
        P(None, row, col),
        P(None, col),
        P(None, col, row),
        P(),
        P(),
        P(),
    )
    out_specs = (
        P(ANY_AXES, None),
        P(ANY_AXES, None),
        P(None, row, col),
        P(None, col),
        P(None, col, row),
        P(),
        P(),
        P(),
        P(None, row, col),
        P(None, col),
        P(None, col, row),
        P(),
        P(),
        P(),
    )
    return jax.shard_map(shards, mesh=fine, in_specs=in_specs, out_specs=out_specs, check_vma=False)
```
